32 devices in a mesh: grp: 2 (over y), gx: 4 (over z), gy: 2 (over x), gz: 2 (over core).
Axes of the slice: x: 2, y: 2, z: 4, core: 2. Of those that a mesh axis runs over, the one named last changes fastest.
Arguments:
- inputs: bfloat16 [2048, 6144], P(('grp', 'gz', 'gy'), 'gx'), parts along dimension 0, may hold values from -6 to 6
- weight: bfloat16 [6144, 24576], P(('gx', 'gz'), 'gy'), may hold values from -0.078125 to 0.078125
- bias: bfloat16 [24576], P('gy'), may hold values from -5 to 5
- cotangent: bfloat16 [2048, 24576], P(('grp', 'gz', 'gx'), 'gy'), parts along dimension 0, may hold values from -0.75 to 0.75
Outputs:
- input_grad: bfloat16 [2048, 6144], P(('grp', 'gz', 'gy'), 'gx'), parts along dimension 0
- weight_grad: bfloat16 [12288, 24576], P(('grp', 'gx', 'gz'), 'gy'), parts along dimension 0
- bias_grad: float32 [49152], P(('grp', 'gy')), parts along dimension 0
The draws below stay inside these ranges and needn't reach their ends.
There are 2 independent parts, one for each index of `grp`. The reference program is written for one: setup_inputs(seed, part) draws one part's arguments, and reference() takes and returns one part's arrays. A program takes and returns all parts, laid end to end along the dimension named above; an argument that names none is the same for every part. Nothing has to cross between parts.
All inputs are finite; a program needn't handle non-finite values.
Results may differ from the reference program's by a relative error of at most 0.011.
Values may be sent and summed in bfloat16 or wider, within the bound.
No kernel may reach another device: no remote copies, remote signals or barrier semaphores. Data moves between devices by JAX's collectives and lax.ppermute only.
A program may use at most 256 MiB of HBM per device.

```python
import jax
import jax.numpy as jnp
from jax import lax

D = 6144
FF = 24576
ROWS = 512
TOKENS = 1024
N_GX = 4
N_GY = 2
N_GZ = 2


def levels(stream_key, dims, shards, low, largest):
    factor_of, own = 1.0, jax.random.fold_in(stream_key, 6)
    for dim, blocks in shards:
        steps = jnp.exp(jax.random.uniform(jax.random.fold_in(own, dim), (blocks,), jnp.float32, low / len(shards), largest / len(shards)))
        factor_of = factor_of * jnp.repeat(steps, dims[dim] // blocks).reshape([-1 if axis == dim else 1 for axis in range(len(dims))])
    return factor_of


def bell_draw(rng, shape, scale, most, shards=(), kind=jnp.bfloat16):
    entries = jax.random.normal(rng, shape, jnp.float32) * scale
    if len(shards) > 0:
        entries = levels(rng, shape, shards, -0.22, 0.18) * entries
    return jnp.clip(entries, min=-most, max=most).astype(kind)


def setup_inputs(seed: int = 0, part: int = 0) -> dict:
    splits = jax.random.split(jax.random.key(seed), 5)
    part_keys = jax.random.split(jax.random.fold_in(splits[4], part), 5)
    inputs = bell_draw(part_keys[0], (TOKENS, D), 1.0, 6.0, ((0, 4), (1, 4)))
    weight = bell_draw(splits[1], (D, FF), D ** -0.5, 0.078125, ((0, 8), (1, 2)))
    bias = bell_draw(splits[2], (FF,), 1.0, 5.0, ((0, 2),))
    cotangent = bell_draw(part_keys[3], (TOKENS, FF), (ROWS // 8) ** -0.5, 0.75, ((0, 8), (1, 2)))
    return dict(inputs=inputs, weight=weight, bias=bias, cotangent=cotangent)


def gelu_slope(preact):
    scale = 0.7978845608028654
    inner = scale * (preact + 0.044715 * preact * preact * preact)
    bend = jnp.tanh(inner)
    return 0.5 * (1.0 + bend) + 0.5 * preact * (1.0 - bend * bend) * scale * (1.0 + 3.0 * 0.044715 * preact * preact)


def rounded(term):
    return lax.optimization_barrier(term.astype(jnp.bfloat16)).astype(jnp.float32)


def reference(inputs, weight, bias, cotangent):
    width = D // N_GX
    preact = jnp.zeros((TOKENS, FF), jnp.float32)
    for block in range(N_GX):
        term = jnp.dot(inputs[:, block * width:(block + 1) * width], weight[block * width:(block + 1) * width, :], preferred_element_type=jnp.float32)
        preact = preact + rounded(term)
    preact = preact + bias.astype(jnp.float32)
    pre_grad = (cotangent.astype(jnp.float32) * gelu_slope(preact)).astype(jnp.bfloat16)
    bias_grad = jnp.sum(pre_grad.astype(jnp.float32), axis=0)
    hidden = FF // N_GY
    input_sum = jnp.zeros((TOKENS, D), jnp.float32)
    columns = []
    for block in range(N_GY):
        grad_cols = pre_grad[:, block * hidden:(block + 1) * hidden]
        weight_cols = weight[:, block * hidden:(block + 1) * hidden]
        term = lax.dot_general(grad_cols, weight_cols, (((1,), (1,)), ((), ())), preferred_element_type=jnp.float32)
        input_sum = input_sum + rounded(term)
        weight_sum = jnp.zeros((D, hidden), jnp.float32)
        for half in range(N_GZ):
            rows_in = inputs[half * ROWS:(half + 1) * ROWS, :]
            rows_grad = grad_cols[half * ROWS:(half + 1) * ROWS, :]
            piece = lax.dot_general(rows_in, rows_grad, (((0,), (0,)), ((), ())), preferred_element_type=jnp.float32)
            weight_sum = weight_sum + rounded(piece)
        columns.append(weight_sum.astype(jnp.bfloat16))
    input_grad = input_sum.astype(jnp.bfloat16)
    weight_grad = jnp.concatenate(columns, axis=1)
    return input_grad, weight_grad, bias_grad
```

```python
import functools

import jax
import jax.numpy as jnp
from jax import lax
from jax.sharding import PartitionSpec as P

F32, BF16 = jnp.float32, jnp.bfloat16


def gelu_slope(preact):
    scale = 0.7978845608028654
    inner = scale * (preact + 0.044715 * preact * preact * preact)
    bend = jnp.tanh(inner)
    return 0.5 * (1.0 + bend) + 0.5 * preact * (1.0 - bend * bend) * scale * (
        1.0 + 3.0 * 0.044715 * preact * preact
    )


def by_core(core, first, second):
    return jnp.where(core == 0, first, second)


def swap(value, axis):
    return lax.ppermute(value, axis, [(0, 1), (1, 0)])


def gather_tokens(inputs, nx, ny, core):
    rows, features = inputs.shape
    if ny == 2:
        side = lax.axis_index("gy")
        beside = swap(inputs, "gy")
        other = swap(inputs, "gz")
        other_beside = swap(beside, "gz")
        mine = jnp.concatenate([by_core(side, inputs, beside), by_core(side, beside, inputs)])
        theirs = jnp.concatenate([by_core(side, other, other_beside), by_core(side, other_beside, other)])
    else:
        mine = lax.all_gather(inputs, "gy", axis=0, tiled=True)
        theirs = swap(mine, "gz")
    both = jnp.stack([by_core(core, mine, theirs), by_core(core, theirs, mine)])
    both = both.reshape(2, nx, rows * ny // nx, features).transpose(1, 0, 2, 3)
    return both.reshape(2 * rows * ny, features)


def pieces(half, nx):
    count = 8 if nx <= 4 else 2
    width = half // count
    return [(c * width, width) for c in range(count)]


def after(value, *others):
    return lax.optimization_barrier((value, *others))[0] if others else value


class Line:
    def __init__(self, n, rank, block):
        self.n, self.rank, self.block = n, rank, block

    def first(self, partial):
        n, rank, block = self.n, self.rank, self.block
        self.partial, self.width = partial, partial.shape[1]
        self.received, self.sums = None, []
        return self.reduce_send(0)

    def reduce_send(self, s):
        n, rank, block = self.n, self.rank, self.block
        size = (n - 1 - s) * block
        start = jnp.where(rank == s, (s + 1) * block, 0)
        send = lax.dynamic_slice(self.partial, (start, 0), (size, self.width))
        if s > 0:
            came = lax.dynamic_slice(self.received, (jnp.where(rank == s, block, 0), 0), (size, self.width))
            send = (send.astype(F32) + came.astype(F32)).astype(BF16)
        return send

    def reduce_permute(self, s, send):
        n = self.n
        self.received = lax.ppermute(send, "gx", [(s, s + 1), (n - 1 - s, n - 2 - s)])
        self.sums.append(self.received)

    def reduced(self):
        n, rank, block = self.n, self.rank, self.block
        own = lax.dynamic_slice(self.partial, (rank * block, 0), (block, self.width)).astype(F32)
        for s, received in enumerate(self.sums):
            size = (n - 1 - s) * block
            own = own + jnp.where(rank == s + 1, received[:block], 0).astype(F32)
            own = own + jnp.where(rank == n - 2 - s, received[size - block :], 0).astype(F32)
        return own

    def gather_first(self, own):
        n, rank, block = self.n, self.rank, self.block
        whole = jnp.zeros((n * block, self.width), own.dtype)
        self.whole = lax.dynamic_update_slice(whole, own, (rank * block, 0))
        return own

    def gather_send(self, u):
        n, rank, block = self.n, self.rank, self.block
        size = (u + 1) * block
        return lax.dynamic_slice(
            self.whole, (jnp.where(rank == u, 0, (n - 1 - u) * block), 0), (size, self.width)
        )

    def gather_permute(self, u, send):
        n = self.n
        self.received = lax.ppermute(send, "gx", [(u, u + 1), (n - 1 - u, n - 2 - u)])

    def gather_place(self, u):
        n, rank, block = self.n, self.rank, self.block
        size = (u + 1) * block
        start = jnp.where(rank == u + 1, 0, (n - 1 - u) * block)
        takes = (rank == u + 1) | (rank == n - 2 - u)
        kept = lax.dynamic_slice(self.whole, (start, 0), (size, self.width))
        whole = jnp.where(takes, self.received, kept)
        self.whole = lax.dynamic_update_slice(self.whole, whole, (start, 0))


def shards(inputs, weight, bias, cotangent, *, nx, ny):
    core, rank = lax.axis_index("gz"), lax.axis_index("gx")
    rows, features = inputs.shape
    mine, hidden = weight.shape
    half = hidden // 2
    block = 2 * rows * ny // nx

    def halves(value, start, width):
        left, right = value[..., start : start + width], value[..., half + start : half + start + width]
        return by_core(core, left, right), by_core(core, right, left)

    tokens = gather_tokens(inputs, nx, ny, core)
    tokens = jnp.concatenate(
        [
            by_core(core, tokens[:, :mine], tokens[:, mine:]),
            by_core(core, tokens[:, mine:], tokens[:, :mine]),
        ],
        axis=1,
    )
    cot_own, cot_send = halves(cotangent, 0, half)
    cot_other = swap(cot_send, "gz")
    cot = jnp.concatenate([by_core(core, cot_own, cot_other), by_core(core, cot_other, cot_own)])
    bias_own, _ = halves(bias, 0, half)
    bias_own = bias_own.astype(F32)

    weight_grad = jnp.zeros((mine, hidden), BF16)
    input_sum = jnp.zeros((tokens.shape[0], features), F32)
    chunks = pieces(half, nx)
    count, steps = len(chunks), nx - 1
    lines = [Line(nx, rank, block) for _ in chunks]
    bias_sums, weights, sends = [], {}, {}
    last = []

    def ordered(value):
        return after(value, *last)

    def note(*values):
        last[:] = values

    def multiply(c):
        start, width = chunks[c]
        w_own, w_send = halves(weight, start, width)
        w = jnp.concatenate([w_own, swap(w_send, "gz")])
        weights[c] = w
        partial = jnp.dot(tokens, ordered(w), preferred_element_type=F32).astype(BF16)
        sends[c] = lines[c].first(partial)
        note(sends[c])

    def reduce_start(c):
        lines[c].reduce_permute(0, ordered(sends[c]))

    def reduce_next(c, s):
        lines[c].received = ordered(lines[c].received)
        send = lines[c].reduce_send(s)
        note(send)
        lines[c].reduce_permute(s, send)

    def slope(c):
        start, width = chunks[c]
        lines[c].sums[-1] = ordered(lines[c].sums[-1])
        preact = lines[c].reduced() + bias_own[start : start + width]
        grad = (cot[:, start : start + width].astype(F32) * gelu_slope(preact)).astype(BF16)
        note(grad)
        lines[c].gather_permute(0, lines[c].gather_first(grad))

    def gather_next(c, u):
        lines[c].received = ordered(lines[c].received)
        lines[c].gather_place(u - 1)
        send = lines[c].gather_send(u)
        note(send)
        lines[c].gather_permute(u, send)

    def use(c):
        nonlocal weight_grad, input_sum
        start, width = chunks[c]
        lines[c].received = ordered(lines[c].received)
        lines[c].gather_place(steps - 1)
        grad = lines[c].whole
        bias_sums.append(jnp.sum(grad, axis=0, dtype=F32))
        w_grad = lax.dot_general(tokens, grad, (((0,), (0,)), ((), ())), preferred_element_type=F32).astype(BF16)
        w_own, w_other = w_grad[:mine], swap(w_grad[mine:], "gz")
        input_sum = input_sum + lax.dot_general(
            grad, weights[c], (((1,), (1,)), ((), ())), preferred_element_type=F32
        )
        note(w_grad, input_sum)
        weight_grad = weight_grad.at[:, start : start + width].set(by_core(core, w_own, w_other))
        weight_grad = weight_grad.at[:, half + start : half + start + width].set(by_core(core, w_other, w_own))

    def do(step, c, *rest):
        if 0 <= c < count:
            step(c, *rest)

    if nx == 4:
        do(multiply, 0)
        for i in range(count + 4):
            do(reduce_start, i)
            do(gather_next, i - 2, 1)
            do(reduce_next, i - 1, 2)
            do(multiply, i + 1)
            do(use, i - 4)
            do(slope, i - 1)
            do(gather_next, i - 2, 2)
            do(reduce_next, i, 1)
    else:
        for c in range(count):
            multiply(c)
            reduce_start(c)
            for s in range(1, steps):
                reduce_next(c, s)
            slope(c)
            for u in range(1, steps):
                gather_next(c, u)
            use(c)

    bias_own = jnp.concatenate(bias_sums)
    bias_other = swap(bias_own, "gz")
    bias_grad = jnp.concatenate([by_core(core, bias_own, bias_other), by_core(core, bias_other, bias_own)])

    input_sum = jnp.concatenate(
        [
            by_core(core, input_sum[:, :mine], input_sum[:, mine:]),
            by_core(core, input_sum[:, mine:], input_sum[:, :mine]),
        ],
        axis=1,
    )
    by_token = input_sum.reshape(nx, 2, block // 2, features)
    kept = by_core(core, by_token[:, 0], by_token[:, 1]).reshape(rows * ny, features)
    sent = by_core(core, by_token[:, 1], by_token[:, 0]).reshape(rows * ny, features)
    term = kept + swap(sent.astype(BF16), "gz").astype(F32)
    if ny == 2:
        side = lax.axis_index("gy")
        kept = by_core(side, term[:rows], term[rows:])
        sent = by_core(side, term[rows:], term[:rows])
        input_grad = (kept + swap(sent.astype(BF16), "gy").astype(F32)).astype(BF16)
    else:
        input_grad = lax.psum_scatter(term.astype(BF16), "gy", scatter_dimension=0, tiled=True)
    return input_grad, weight_grad, bias_grad


def solution(mesh):
    placed = (
        P(("grp", "gz", "gy"), "gx"),
        P(("gx", "gz"), "gy"),
        P("gy"),
        P(("grp", "gz", "gx"), "gy"),
    )
    return jax.shard_map(
        functools.partial(shards, nx=mesh.shape["gx"], ny=mesh.shape["gy"]),
        mesh=mesh,
        in_specs=placed,
        out_specs=(P(("grp", "gz", "gy"), "gx"), P(("grp", "gx", "gz"), "gy"), P(("grp", "gy"))),
        check_vma=False,
    )
```

```python
import functools

import jax
import jax.numpy as jnp
from jax import lax
from jax.sharding import PartitionSpec as P

F32, BF16 = jnp.float32, jnp.bfloat16


def gelu_slope(preact):
    scale = 0.7978845608028654
    inner = scale * (preact + 0.044715 * preact * preact * preact)
    bend = jnp.tanh(inner)
    return 0.5 * (1.0 + bend) + 0.5 * preact * (1.0 - bend * bend) * scale * (
        1.0 + 3.0 * 0.044715 * preact * preact
    )


def by_core(core, first, second):
    return jnp.where(core == 0, first, second)


def swap(value, axis):
    return lax.ppermute(value, axis, [(0, 1), (1, 0)])


def gather_tokens(inputs, nx, ny, core):
    rows, features = inputs.shape
    if ny == 2:
        side = lax.axis_index("gy")
        beside = swap(inputs, "gy")
        other = swap(inputs, "gz")
        other_beside = swap(beside, "gz")
        mine = jnp.concatenate([by_core(side, inputs, beside), by_core(side, beside, inputs)])
        theirs = jnp.concatenate([by_core(side, other, other_beside), by_core(side, other_beside, other)])
    else:
        mine = lax.all_gather(inputs, "gy", axis=0, tiled=True)
        theirs = swap(mine, "gz")
    both = jnp.stack([by_core(core, mine, theirs), by_core(core, theirs, mine)])
    both = both.reshape(2, nx, rows * ny // nx, features).transpose(1, 0, 2, 3)
    return both.reshape(2 * rows * ny, features)


def pieces(half, nx):
    shares = (1, 1, 1, 1, 1, 1, 1, 1) if nx <= 4 else (1, 1)
    widths = [half * share // sum(shares) for share in shares]
    return [(sum(widths[:c]), widths[c]) for c in range(len(widths))]


def after(value, *others):
    return lax.optimization_barrier((value, *others))[0] if others else value


class Line:
    def __init__(self, n, rank, block):
        self.n, self.rank, self.block = n, rank, block

    def first(self, partial):
        n, rank, block = self.n, self.rank, self.block
        self.partial, self.width = partial, partial.shape[1]
        self.received, self.sums = None, []
        return self.reduce_send(0)

    def reduce_send(self, s):
        n, rank, block = self.n, self.rank, self.block
        size = (n - 1 - s) * block
        start = jnp.where(rank == s, (s + 1) * block, 0)
        send = lax.dynamic_slice(self.partial, (start, 0), (size, self.width))
        if s > 0:
            came = lax.dynamic_slice(self.received, (jnp.where(rank == s, block, 0), 0), (size, self.width))
            send = (send.astype(F32) + came.astype(F32)).astype(BF16)
        return send

    def reduce_permute(self, s, send):
        n = self.n
        self.received = lax.ppermute(send, "gx", [(s, s + 1), (n - 1 - s, n - 2 - s)])
        self.sums.append(self.received)

    def reduced(self):
        n, rank, block = self.n, self.rank, self.block
        own = lax.dynamic_slice(self.partial, (rank * block, 0), (block, self.width)).astype(F32)
        for s, received in enumerate(self.sums):
            size = (n - 1 - s) * block
            own = own + jnp.where(rank == s + 1, received[:block], 0).astype(F32)
            own = own + jnp.where(rank == n - 2 - s, received[size - block :], 0).astype(F32)
        return own

    def gather_first(self, own):
        n, rank, block = self.n, self.rank, self.block
        whole = jnp.zeros((n * block, self.width), own.dtype)
        self.whole = lax.dynamic_update_slice(whole, own, (rank * block, 0))
        return own

    def gather_send(self, u):
        n, rank, block = self.n, self.rank, self.block
        size = (u + 1) * block
        return lax.dynamic_slice(
            self.whole, (jnp.where(rank == u, 0, (n - 1 - u) * block), 0), (size, self.width)
        )

    def gather_permute(self, u, send):
        n = self.n
        self.received = lax.ppermute(send, "gx", [(u, u + 1), (n - 1 - u, n - 2 - u)])

    def gather_place(self, u):
        n, rank, block = self.n, self.rank, self.block
        size = (u + 1) * block
        start = jnp.where(rank == u + 1, 0, (n - 1 - u) * block)
        takes = (rank == u + 1) | (rank == n - 2 - u)
        kept = lax.dynamic_slice(self.whole, (start, 0), (size, self.width))
        whole = jnp.where(takes, self.received, kept)
        self.whole = lax.dynamic_update_slice(self.whole, whole, (start, 0))


def shards(inputs, weight, bias, cotangent, *, nx, ny):
    core, rank = lax.axis_index("gz"), lax.axis_index("gx")
    rows, features = inputs.shape
    mine, hidden = weight.shape
    half = hidden // 2
    block = 2 * rows * ny // nx

    def halves(value, start, width):
        left, right = value[..., start : start + width], value[..., half + start : half + start + width]
        return by_core(core, left, right), by_core(core, right, left)

    tokens = gather_tokens(inputs, nx, ny, core)
    tokens = jnp.concatenate(
        [
            by_core(core, tokens[:, :mine], tokens[:, mine:]),
            by_core(core, tokens[:, mine:], tokens[:, :mine]),
        ],
        axis=1,
    )
    cot_own, cot_send = halves(cotangent, 0, half)
    cot_other = swap(cot_send, "gz")
    cot = jnp.concatenate([by_core(core, cot_own, cot_other), by_core(core, cot_other, cot_own)])
    bias_own, _ = halves(bias, 0, half)
    bias_own = bias_own.astype(F32)

    weight_grad = jnp.zeros((mine, hidden), BF16)
    input_sum = jnp.zeros((tokens.shape[0], features), BF16)
    chunks = pieces(half, nx)
    count, steps = len(chunks), nx - 1
    lines = [Line(nx, rank, block) for _ in chunks]
    bias_sums, weights, sends = [], {}, {}
    last = []

    def ordered(value):
        return after(value, *last)

    def note(*values):
        last[:] = values

    def multiply(c):
        start, width = chunks[c]
        w_own, w_send = halves(weight, start, width)
        w = jnp.concatenate([w_own, swap(w_send, "gz")])
        weights[c] = w
        partial = jnp.dot(tokens, ordered(w), preferred_element_type=F32).astype(BF16)
        sends[c] = lines[c].first(partial)
        note(sends[c])

    def reduce_start(c):
        lines[c].reduce_permute(0, ordered(sends[c]))

    def reduce_next(c, s):
        lines[c].received = ordered(lines[c].received)
        send = lines[c].reduce_send(s)
        note(send)
        lines[c].reduce_permute(s, send)

    def slope(c):
        start, width = chunks[c]
        lines[c].sums[-1] = ordered(lines[c].sums[-1])
        preact = lines[c].reduced() + bias_own[start : start + width]
        grad = (cot[:, start : start + width].astype(F32) * gelu_slope(preact)).astype(BF16)
        note(grad)
        lines[c].gather_permute(0, lines[c].gather_first(grad))

    def gather_next(c, u):
        lines[c].received = ordered(lines[c].received)
        lines[c].gather_place(u - 1)
        send = lines[c].gather_send(u)
        note(send)
        lines[c].gather_permute(u, send)

    def use(c):
        nonlocal weight_grad, input_sum
        start, width = chunks[c]
        lines[c].received = ordered(lines[c].received)
        lines[c].gather_place(steps - 1)
        grad = lines[c].whole
        bias_sums.append(jnp.sum(grad, axis=0, dtype=F32))
        w_grad = lax.dot_general(tokens, grad, (((0,), (0,)), ((), ())), preferred_element_type=F32).astype(BF16)
        w_own, w_other = w_grad[:mine], swap(w_grad[mine:], "gz")
        term = lax.dot_general(grad, weights[c], (((1,), (1,)), ((), ())), preferred_element_type=F32)
        input_sum = (input_sum.astype(F32) + term).astype(BF16)
        note(w_grad, input_sum)
        weight_grad = weight_grad.at[:, start : start + width].set(by_core(core, w_own, w_other))
        weight_grad = weight_grad.at[:, half + start : half + start + width].set(by_core(core, w_other, w_own))

    def do(step, c, *rest):
        if 0 <= c < count:
            step(c, *rest)

    if nx == 4:
        do(multiply, 0)
        for i in range(count + 4):
            do(reduce_start, i)
            do(gather_next, i - 2, 1)
            do(multiply, i + 1)
            do(reduce_next, i - 1, 2)
            do(use, i - 4)
            do(slope, i - 1)
            do(gather_next, i - 2, 2)
            do(reduce_next, i, 1)
    else:
        for c in range(count):
            multiply(c)
            reduce_start(c)
            for s in range(1, steps):
                reduce_next(c, s)
            slope(c)
            for u in range(1, steps):
                gather_next(c, u)
            use(c)

    bias_own = jnp.concatenate(bias_sums)
    bias_other = swap(bias_own, "gz")
    bias_grad = jnp.concatenate([by_core(core, bias_own, bias_other), by_core(core, bias_other, bias_own)])

    input_sum = input_sum.astype(F32)
    input_sum = jnp.concatenate(
        [
            by_core(core, input_sum[:, :mine], input_sum[:, mine:]),
            by_core(core, input_sum[:, mine:], input_sum[:, :mine]),
        ],
        axis=1,
    )
    by_token = input_sum.reshape(nx, 2, block // 2, features)
    kept = by_core(core, by_token[:, 0], by_token[:, 1]).reshape(rows * ny, features)
    sent = by_core(core, by_token[:, 1], by_token[:, 0]).reshape(rows * ny, features)
    term = kept + swap(sent.astype(BF16), "gz").astype(F32)
    if ny == 2:
        side = lax.axis_index("gy")
        kept = by_core(side, term[:rows], term[rows:])
        sent = by_core(side, term[rows:], term[:rows])
        input_grad = (kept + swap(sent.astype(BF16), "gy").astype(F32)).astype(BF16)
    else:
        input_grad = lax.psum_scatter(term.astype(BF16), "gy", scatter_dimension=0, tiled=True)
    return input_grad, weight_grad, bias_grad


def solution(mesh):
    placed = (
        P(("grp", "gz", "gy"), "gx"),
        P(("gx", "gz"), "gy"),
        P("gy"),
        P(("grp", "gz", "gx"), "gy"),
    )
    return jax.shard_map(
        functools.partial(shards, nx=mesh.shape["gx"], ny=mesh.shape["gy"]),
        mesh=mesh,
        in_specs=placed,
        out_specs=(P(("grp", "gz", "gy"), "gx"), P(("grp", "gx", "gz"), "gy"), P(("grp", "gy"))),
        check_vma=False,
    )
```

```python
import functools

import jax
import jax.numpy as jnp
from jax import lax
from jax.sharding import PartitionSpec as P

F32, BF16 = jnp.float32, jnp.bfloat16


def gelu_slope(preact):
    scale = 0.7978845608028654
    inner = scale * (preact + 0.044715 * preact * preact * preact)
    bend = jnp.tanh(inner)
    return 0.5 * (1.0 + bend) + 0.5 * preact * (1.0 - bend * bend) * scale * (
        1.0 + 3.0 * 0.044715 * preact * preact
    )


def by_core(core, first, second):
    return jnp.where(core == 0, first, second)


def swap(value, axis):
    return lax.ppermute(value, axis, [(0, 1), (1, 0)])


def gather_tokens(inputs, nx, ny, core):
    rows, features = inputs.shape
    if ny == 2:
        side = lax.axis_index("gy")
        beside = swap(inputs, "gy")
        other = swap(inputs, "gz")
        other_beside = swap(beside, "gz")
        mine = jnp.concatenate([by_core(side, inputs, beside), by_core(side, beside, inputs)])
        theirs = jnp.concatenate([by_core(side, other, other_beside), by_core(side, other_beside, other)])
    else:
        mine = lax.all_gather(inputs, "gy", axis=0, tiled=True)
        theirs = swap(mine, "gz")
    both = jnp.stack([by_core(core, mine, theirs), by_core(core, theirs, mine)])
    both = both.reshape(2, nx, rows * ny // nx, features).transpose(1, 0, 2, 3)
    return both.reshape(2 * rows * ny, features)


def pieces(half, nx):
    shares = (1, 1, 1, 1, 1, 1, 1, 1) if nx <= 4 else (1, 1)
    widths = [half * share // sum(shares) for share in shares]
    return [(sum(widths[:c]), widths[c]) for c in range(len(widths))]


def after(value, *others):
    return lax.optimization_barrier((value, *others))[0] if others else value


class Line:
    def __init__(self, n, rank, block):
        self.n, self.rank, self.block = n, rank, block

    def first(self, partial):
        n, rank, block = self.n, self.rank, self.block
        self.partial, self.width = partial, partial.shape[1]
        self.received, self.sums = None, []
        return self.reduce_send(0)

    def reduce_send(self, s):
        n, rank, block = self.n, self.rank, self.block
        size = (n - 1 - s) * block
        start = jnp.where(rank == s, (s + 1) * block, 0)
        send = lax.dynamic_slice(self.partial, (start, 0), (size, self.width))
        if s > 0:
            came = lax.dynamic_slice(self.received, (jnp.where(rank == s, block, 0), 0), (size, self.width))
            send = (send.astype(F32) + came.astype(F32)).astype(BF16)
        return send

    def reduce_permute(self, s, send):
        n = self.n
        self.received = lax.ppermute(send, "gx", [(s, s + 1), (n - 1 - s, n - 2 - s)])
        self.sums.append(self.received)

    def reduced(self):
        n, rank, block = self.n, self.rank, self.block
        own = lax.dynamic_slice(self.partial, (rank * block, 0), (block, self.width)).astype(F32)
        for s, received in enumerate(self.sums):
            size = (n - 1 - s) * block
            own = own + jnp.where(rank == s + 1, received[:block], 0).astype(F32)
            own = own + jnp.where(rank == n - 2 - s, received[size - block :], 0).astype(F32)
        return own

    def gather_first(self, own):
        n, rank, block = self.n, self.rank, self.block
        whole = jnp.zeros((n * block, self.width), own.dtype)
        self.whole = lax.dynamic_update_slice(whole, own, (rank * block, 0))
        return own

    def gather_send(self, u):
        n, rank, block = self.n, self.rank, self.block
        size = (u + 1) * block
        return lax.dynamic_slice(
            self.whole, (jnp.where(rank == u, 0, (n - 1 - u) * block), 0), (size, self.width)
        )

    def gather_permute(self, u, send):
        n = self.n
        self.received = lax.ppermute(send, "gx", [(u, u + 1), (n - 1 - u, n - 2 - u)])

    def gather_place(self, u):
        n, rank, block = self.n, self.rank, self.block
        size = (u + 1) * block
        start = jnp.where(rank == u + 1, 0, (n - 1 - u) * block)
        takes = (rank == u + 1) | (rank == n - 2 - u)
        kept = lax.dynamic_slice(self.whole, (start, 0), (size, self.width))
        whole = jnp.where(takes, self.received, kept)
        self.whole = lax.dynamic_update_slice(self.whole, whole, (start, 0))


def shards(inputs, weight, bias, cotangent, *, nx, ny):
    core, rank = lax.axis_index("gz"), lax.axis_index("gx")
    rows, features = inputs.shape
    mine, hidden = weight.shape
    half = hidden // 2
    block = 2 * rows * ny // nx

    def halves(value, start, width):
        left, right = value[..., start : start + width], value[..., half + start : half + start + width]
        return by_core(core, left, right), by_core(core, right, left)

    tokens = gather_tokens(inputs, nx, ny, core)
    tokens = jnp.concatenate(
        [
            by_core(core, tokens[:, :mine], tokens[:, mine:]),
            by_core(core, tokens[:, mine:], tokens[:, :mine]),
        ],
        axis=1,
    )
    cot_own, cot_send = halves(cotangent, 0, half)
    cot_other = swap(cot_send, "gz")
    cot = jnp.concatenate([by_core(core, cot_own, cot_other), by_core(core, cot_other, cot_own)])
    bias_own, _ = halves(bias, 0, half)
    bias_own = bias_own.astype(F32)

    weight_grad = jnp.zeros((mine, hidden), BF16)
    input_sum = jnp.zeros((tokens.shape[0], features), BF16)
    chunks = pieces(half, nx)
    count, steps = len(chunks), nx - 1
    lines = [Line(nx, rank, block) for _ in chunks]
    bias_sums, weights, sends = [], {}, {}
    last = []

    def ordered(value):
        return after(value, *last)

    def note(*values):
        last[:] = values

    def multiply(c):
        start, width = chunks[c]
        w_own, w_send = halves(weight, start, width)
        w = jnp.concatenate([w_own, swap(w_send, "gz")])
        weights[c] = w
        partial = jnp.dot(tokens, ordered(w), preferred_element_type=F32).astype(BF16)
        sends[c] = lines[c].first(partial)
        note(sends[c])

    def reduce_start(c):
        lines[c].reduce_permute(0, ordered(sends[c]))

    def reduce_next(c, s):
        lines[c].received = ordered(lines[c].received)
        send = lines[c].reduce_send(s)
        note(send)
        lines[c].reduce_permute(s, send)

    def slope(c):
        start, width = chunks[c]
        lines[c].sums[-1] = ordered(lines[c].sums[-1])
        preact = lines[c].reduced() + bias_own[start : start + width]
        grad = (cot[:, start : start + width].astype(F32) * gelu_slope(preact)).astype(BF16)
        note(grad)
        lines[c].gather_permute(0, lines[c].gather_first(grad))

    def gather_next(c, u):
        lines[c].received = ordered(lines[c].received)
        lines[c].gather_place(u - 1)
        send = lines[c].gather_send(u)
        note(send)
        lines[c].gather_permute(u, send)

    def use(c):
        nonlocal weight_grad, input_sum
        start, width = chunks[c]
        lines[c].received = ordered(lines[c].received)
        lines[c].gather_place(steps - 1)
        grad = lines[c].whole
        bias_sums.append(jnp.sum(grad, axis=0, dtype=F32))
        term = lax.dot_general(grad, weights[c], (((1,), (1,)), ((), ())), preferred_element_type=F32)
        input_sum = (input_sum.astype(F32) + term).astype(BF16)
        w_rows = after(grad, input_sum) if c + 1 == count else grad
        w_grad = lax.dot_general(tokens, w_rows, (((0,), (0,)), ((), ())), preferred_element_type=F32).astype(BF16)
        w_own, w_other = w_grad[:mine], swap(w_grad[mine:], "gz")
        note(w_grad, input_sum)
        weight_grad = weight_grad.at[:, start : start + width].set(by_core(core, w_own, w_other))
        weight_grad = weight_grad.at[:, half + start : half + start + width].set(by_core(core, w_other, w_own))

    def do(step, c, *rest):
        if 0 <= c < count:
            step(c, *rest)

    if nx == 4:
        do(multiply, 0)
        for i in range(count + 4):
            do(reduce_start, i)
            do(gather_next, i - 2, 1)
            do(multiply, i + 1)
            do(reduce_next, i - 1, 2)
            do(use, i - 4)
            do(slope, i - 1)
            do(gather_next, i - 2, 2)
            do(reduce_next, i, 1)
    else:
        for c in range(count):
            multiply(c)
            reduce_start(c)
            for s in range(1, steps):
                reduce_next(c, s)
            slope(c)
            for u in range(1, steps):
                gather_next(c, u)
            use(c)

    bias_own = jnp.concatenate(bias_sums)
    bias_other = swap(bias_own, "gz")
    bias_grad = jnp.concatenate([by_core(core, bias_own, bias_other), by_core(core, bias_other, bias_own)])

    input_sum = input_sum.astype(F32)
    input_sum = jnp.concatenate(
        [
            by_core(core, input_sum[:, :mine], input_sum[:, mine:]),
            by_core(core, input_sum[:, mine:], input_sum[:, :mine]),
        ],
        axis=1,
    )
    by_token = input_sum.reshape(nx, 2, block // 2, features)
    kept = by_core(core, by_token[:, 0], by_token[:, 1]).reshape(rows * ny, features)
    sent = by_core(core, by_token[:, 1], by_token[:, 0]).reshape(rows * ny, features)
    term = kept + swap(sent.astype(BF16), "gz").astype(F32)
    if ny == 2:
        side = lax.axis_index("gy")
        kept = by_core(side, term[:rows], term[rows:])
        sent = by_core(side, term[rows:], term[:rows])
        input_grad = (kept + swap(sent.astype(BF16), "gy").astype(F32)).astype(BF16)
    else:
        input_grad = lax.psum_scatter(term.astype(BF16), "gy", scatter_dimension=0, tiled=True)
    return input_grad, weight_grad, bias_grad


def solution(mesh):
    placed = (
        P(("grp", "gz", "gy"), "gx"),
        P(("gx", "gz"), "gy"),
        P("gy"),
        P(("grp", "gz", "gx"), "gy"),
    )
    return jax.shard_map(
        functools.partial(shards, nx=mesh.shape["gx"], ny=mesh.shape["gy"]),
        mesh=mesh,
        in_specs=placed,
        out_specs=(P(("grp", "gz", "gy"), "gx"), P(("grp", "gx", "gz"), "gy"), P(("grp", "gy"))),
        check_vma=False,
    )
```
